32 devices in a mesh: grp: 2 (over y), lat: 4 (over z), ch: 2 (over x), lon: 2 (over core).
Axes of the slice: x: 2, y: 2, z: 4, core: 2. Of those that a mesh axis runs over, the one named last changes fastest.
Arguments:
- grad_out: bfloat16 [384, 16, 1024], P('ch', ('grp', 'lat'), 'lon'), parts along dimension 1, may hold values from -6 to 6
- saved_basis: bfloat16 [9, 384, 16, 1024], P(None, 'ch', ('grp', 'lat'), 'lon'), parts along dimension 2, may hold values from -6 to 6
- weight: bfloat16 [384, 9, 384], P(None, None, 'ch'), may hold values from -0.109375 to 0.109375
- quad_tiles: bfloat16 [8, 16, 9, 64, 64], P('lat'), may hold values from -0.25 to 0.25
- col_rows: int32 [8, 16], P('lat'), may hold values from 0 to 7, as said below
- col_shift: int32 [8, 16], P('lat'), may hold values from 0 to 15
- block_count: int32 [8], P('lat'), may hold values from 2 to 16, as said below
Outputs:
- grad_input: float32 [384, 16, 1024], P('ch', ('grp', 'lat'), 'lon'), parts along dimension 1
- grad_weight: float32 [768, 9, 384], P(('grp', 'lat', 'lon'), None, 'ch'), parts along dimension 0
The draws below stay inside these ranges and needn't reach their ends.
There are 2 independent parts, one for each index of `grp`. The reference program is written for one: setup_inputs(seed, part) draws one part's arguments, and reference() takes and returns one part's arrays. A program takes and returns all parts, laid end to end along the dimension named above; an argument that names none is the same for every part. Nothing has to cross between parts.
Inputs may be any that keep to these rules, and one draw needn't show every extreme that they name: `col_rows`: each entry's input row lies within 4 rows of its own row. `block_count`: entries at or past a row's count are not used.
All inputs are finite; a program needn't handle non-finite values.
Results may differ from the reference program's by a relative error of at most 0.0029.
Values may be sent and summed in bfloat16 or wider, within the bound.
A program may use at most 128 MiB of HBM per device.

```python
import jax
import jax.numpy as jnp
from jax import lax

C = 384
K = 9
NE = 16
HALO_DEV = 2
ROWS_DEV = 2
NLAT = 8
NLON = 1024


def draw_col_rows(key, part):
    key = jax.random.fold_in(key, 11)
    reach_rows = HALO_DEV * ROWS_DEV
    own_rows = jnp.arange(NLAT, dtype=jnp.int32)[:, None]
    entry_ids = jnp.arange(NE, dtype=jnp.int32)[None, :]
    offsets = jax.random.randint(key, (NLAT, NE), -reach_rows, reach_rows + 1, dtype=jnp.int32)
    offsets = jnp.where(entry_ids == 0, 0, offsets)
    offsets = jnp.where(entry_ids == 1, reach_rows, offsets)
    offsets = jnp.where(entry_ids == 2, -reach_rows, offsets)
    return jnp.clip(own_rows + offsets, 0, NLAT - 1).astype(jnp.int32)


def draw_block_count(key, part):
    key = jax.random.fold_in(key, 12)
    first_key, second_key = jax.random.split(key)
    row_ids = jnp.arange(NLAT, dtype=jnp.int32)
    distance = jnp.minimum(row_ids, NLAT - 1 - row_ids)
    first_draw = jax.random.randint(first_key, (NLAT,), 2, NE + 1, dtype=jnp.int32)
    second_draw = jax.random.randint(second_key, (NLAT,), 2, NE + 1, dtype=jnp.int32)
    polar = distance * 4 < NLAT
    counts = jnp.where(polar, jnp.maximum(first_draw, second_draw), first_draw)
    counts = jnp.where(row_ids == 0, NE, counts)
    counts = jnp.where(row_ids == NLAT // 2, 2, counts)
    return counts.astype(jnp.int32)


def set_ends(drawn, stream_key, least, high):
    shape = drawn.shape
    place = [jax.random.randint(jax.random.fold_in(stream_key, axis), (), 0, shape[axis]) for axis in range(len(shape))]
    drawn = drawn.at[tuple(place)].set(least)
    longest = shape.index(max(shape))
    place[longest] = (place[longest] + 1) % shape[longest]
    return drawn.at[tuple(place)].set(high)


def with_spikes(result, own_key, source, target, parts, factor):
    def block_of(axis_at):
        return (jnp.arange(result.shape[axis_at]) // (result.shape[axis_at] // parts)).reshape((-1,) + (1,) * (result.ndim - 1 - axis_at))

    near = jax.random.permutation(own_key, parts)[block_of(target)]
    second = (block_of(target) + parts // 2) % parts
    return jnp.where((block_of(source) == near) | (block_of(source) == second), factor * result, result)


def levels(own_key, extent, cuts, low, high):
    def one(position, parts):
        steps = jax.random.uniform(jax.random.fold_in(jax.random.fold_in(own_key, 6), position), (parts,), jnp.float32, low / len(cuts), high / len(cuts))
        return jnp.repeat(jnp.exp(steps), extent[position] // parts).reshape((-1,) + (1,) * (len(extent) - position - 1))

    gain = one(*cuts[0])
    for cut in cuts[1:]:
        gain = gain * one(*cut)
    return gain


def noise(key, extent, scale, bound, cuts=(), held_as=jnp.bfloat16):
    loudness = levels(key, extent, cuts, -0.22, 0.18) if cuts else 1.0
    values = jax.random.normal(key, extent, jnp.float32) * scale * loudness
    return jnp.minimum(jnp.maximum(values, -bound), bound).astype(held_as)


def bell_draw_with(key, extent, deviation, most, cuts, heavy, kind=jnp.bfloat16):
    values = deviation * jax.random.normal(key, extent, jnp.float32)
    if cuts:
        values = values * levels(key, extent, cuts, -0.22, 0.18)
    return jnp.clip(with_spikes(values, jax.random.fold_in(key, 3), *heavy), -most, most).astype(kind)


def setup_inputs(seed: int = 0, part: int = 0) -> dict:
    key_of = jax.random.split(jax.random.key(seed), 8)
    own_keys = jax.random.split(jax.random.fold_in(key_of[7], part), 8)
    return {
        "grad_out": bell_draw_with(own_keys[0], (C, NLAT, NLON), 1.0, 6.0, ((0, 2), (1, 4), (2, 2)), (1, 0, 4, 2.0)),
        "saved_basis": noise(own_keys[1], (K, C, NLAT, NLON), 1.0, 6.0, ((1, 2), (2, 4), (3, 2))),
        "weight": noise(key_of[2], (C, K, C), (C * K) ** -0.5, 0.109375, ((2, 2),)),
        "quad_tiles": noise(key_of[3], (NLAT, NE, K, 64, 64), (K * 64) ** -0.5, 0.25, ((0, 4),)),
        "col_rows": draw_col_rows(jax.random.fold_in(key_of[7], 71), part),
        "col_shift": set_ends(jax.random.randint(key_of[5], (NLAT, NE), 0, NLON // 64), jax.random.fold_in(key_of[5], 1), 0, (NLON // 64) - 1).astype(jnp.int32),
        "block_count": draw_block_count(jax.random.fold_in(key_of[7], 71), part),
    }


def reference(grad_out, saved_basis, weight, quad_tiles, col_rows, col_shift, block_count):
    channels, lat_rows, cycle_len = grad_out.shape
    basis_count = saved_basis.shape[0]
    blocks = cycle_len // 64
    entries = quad_tiles.shape[1]
    flat_out = grad_out.reshape(channels, lat_rows * cycle_len)
    flat_basis = saved_basis.reshape(basis_count * channels, lat_rows * cycle_len)
    grad_weight = lax.dot_general(flat_out, flat_basis, (((1,), (1,)), ((), ())), preferred_element_type=jnp.float32)
    grad_weight = grad_weight.reshape(channels, basis_count, channels)
    mixing = weight.reshape(channels, basis_count * channels)

    def one_row(row_index, summed):
        out_row = lax.dynamic_index_in_dim(grad_out, row_index, 1, keepdims=False)
        mixed_grad = lax.dot_general(mixing, out_row, (((0,), (0,)), ((), ())), preferred_element_type=jnp.float32).astype(jnp.bfloat16)
        mixed_grad = mixed_grad.reshape(basis_count, channels, blocks, 64).astype(jnp.float32)
        row_tiles = lax.dynamic_index_in_dim(quad_tiles, row_index, 0, keepdims=False).astype(jnp.float32)
        pieces = jnp.einsum("kcjp,ekpq->ecjq", mixed_grad, row_tiles).reshape(entries, channels, cycle_len)
        targets = lax.dynamic_index_in_dim(col_rows, row_index, 0, keepdims=False)
        shifts = lax.dynamic_index_in_dim(col_shift, row_index, 0, keepdims=False)
        live_count = lax.dynamic_index_in_dim(block_count, row_index, 0, keepdims=False)
        for entry_id in range(entries):
            rolled = jnp.roll(pieces[entry_id], shifts[entry_id] * 64, axis=1)
            live_weight = (live_count > entry_id).astype(rolled.dtype)
            current = lax.dynamic_index_in_dim(summed, targets[entry_id], 1, keepdims=False)
            summed = lax.dynamic_update_index_in_dim(summed, current + live_weight * rolled, targets[entry_id], 1)
        return summed

    grad_input = lax.fori_loop(0, lat_rows, one_row, jnp.zeros((channels, lat_rows, cycle_len), jnp.float32))
    return grad_input, grad_weight
```

```python
import functools

import jax
import jax.numpy as jnp
from jax import lax
from jax.experimental import pallas as pl
from jax.experimental.pallas import tpu as pltpu
from jax.sharding import PartitionSpec as P

HALO_DEV = 2
BLOCK = 64
LANES = 128


def quadrature_kernel(
    own_half, target, shift, lon, g_ref, w_ref, t_ref, far_ref, near_ref, acc, mixed, piece
):
    lon_halves, groups, rows, _, width = g_ref.shape
    window, cycle_blocks = acc.shape[0] - 1, acc.shape[1]
    entries = target.shape[1]
    basis = w_ref.shape[2] // LANES
    blocks = width // BLOCK
    pairs = cycle_blocks // 2
    acc[...] = jnp.zeros_like(acc)
    for row in range(rows):
        for half in range(lon_halves):
            total = None
            for group in range(groups):
                term = lax.dot_general(
                    g_ref[half, group, row],
                    w_ref[group],
                    (((0,), (0,)), ((), ())),
                    preferred_element_type=jnp.float32,
                )
                total = term if total is None else total + term
            total = total.astype(jnp.bfloat16)
            for block in range(blocks):
                at = half * blocks + block
                for k in range(basis):
                    mixed[
                        at // 2,
                        k * BLOCK : (k + 1) * BLOCK,
                        (at % 2) * LANES : (at % 2 + 1) * LANES,
                    ] = total[block * BLOCK : (block + 1) * BLOCK, k * LANES : (k + 1) * LANES]

        @pl.loop(0, pairs)
        def _(pair):
            piece[...] = jnp.dot(
                t_ref[row], mixed[pair], preferred_element_type=jnp.float32
            )
            for entry in range(entries):
                for side in range(2):
                    place = lax.rem(2 * pair + side + shift[row, entry], cycle_blocks)
                    acc[target[row, entry], place] += piece[
                        entry * BLOCK : (entry + 1) * BLOCK, side * LANES : (side + 1) * LANES
                    ]

    mid = window // rows // 2
    for at in range(window):
        step, row = at // rows, at % rows
        for side in range(2):
            half = lax.rem(lon[0] + side, 2)
            turned = acc[at, pl.ds(half * blocks, blocks)].reshape(width, LANES).T[:own_half]
            if step == mid:
                near_ref[side, row] = turned
            else:
                far_ref[step - (step > mid), side, row] = turned.astype(jnp.bfloat16)


def quadrature(own_half, target, shift, lon, g, w, t, window):
    lon_halves, groups, rows, _, width = g.shape
    cycle_blocks = lon_halves * width // BLOCK
    depth = t.shape[2]
    vmem = pl.BlockSpec(memory_space=pltpu.VMEM)
    smem = pl.BlockSpec(memory_space=pltpu.SMEM)
    return pl.pallas_call(
        functools.partial(quadrature_kernel, own_half),
        out_shape=(
            jax.ShapeDtypeStruct(
                (window // rows - 1, 2, rows, own_half, width), jnp.bfloat16
            ),
            jax.ShapeDtypeStruct((2, rows, own_half, width), jnp.float32),
        ),
        in_specs=[smem, smem, smem, vmem, vmem, vmem],
        out_specs=(vmem, vmem),
        scratch_shapes=[
            pltpu.VMEM((window + 1, cycle_blocks, BLOCK, LANES), jnp.float32),
            pltpu.VMEM((cycle_blocks // 2, depth, 2 * LANES), jnp.bfloat16),
            pltpu.VMEM((t.shape[1], 2 * LANES), jnp.float32),
        ],
        compiler_params=pltpu.CompilerParams(vmem_limit_bytes=48 * 1024 * 1024),
        cost_estimate=pl.CostEstimate(
            flops=9 * 10**9, bytes_accessed=10 * 2**20, transcendentals=0
        ),
    )(target, shift, lon, g, w, t)


def filter_gradient(full_out, saved_basis):
    product = jnp.einsum(
        "crow,kirw->coki", full_out, saved_basis, preferred_element_type=jnp.float32
    )
    groups, per, basis, channels = product.shape
    lat_devices = lax.axis_size("lat")
    lon_devices = lax.axis_size("lon")
    own_rows = groups * per // (lat_devices * lon_devices)
    if lat_devices > 8 or lon_devices != 2:
        return lax.psum_scatter(
            product.reshape(groups * per, basis, channels),
            ("lat", "lon"),
            scatter_dimension=0,
            tiled=True,
        )
    lat = lax.axis_index("lat")
    lon = lax.axis_index("lon")
    product = product.reshape(lat_devices, 2, own_rows, basis, channels)
    kept = lax.dynamic_index_in_dim(product, lon, 1, keepdims=False)
    given = lax.dynamic_index_in_dim(product, 1 - lon, 1, keepdims=False)
    kept = kept + lax.ppermute(given.astype(jnp.bfloat16), "lon", [(0, 1), (1, 0)])
    result = lax.dynamic_index_in_dim(kept, lat, 0, keepdims=False)
    narrow = kept.astype(jnp.bfloat16)
    for step in range(1, lat_devices):
        sent = lax.dynamic_index_in_dim(
            narrow, lax.rem(lat + step, lat_devices), 0, keepdims=False
        )
        result = result + lax.ppermute(
            sent, "lat", [(at, (at + step) % lat_devices) for at in range(lat_devices)]
        )
    return result


def body(grad_out, saved_basis, weight, quad_tiles, col_rows, col_shift, block_count):
    channels, rows, width = grad_out.shape
    basis = saved_basis.shape[0]
    out_channels = weight.shape[0]
    entries = quad_tiles.shape[1]
    lat_devices = lax.axis_size("lat")
    lat = lax.axis_index("lat")
    lon = lax.axis_index("lon")
    groups = out_channels // channels
    own_half = channels // 2
    window = (2 * HALO_DEV + 1) * rows

    full_out = lax.all_gather(grad_out.transpose(1, 0, 2), "ch", axis=0, tiled=False)
    grad_weight = filter_gradient(full_out, saved_basis)

    whole_out = lax.all_gather(full_out, "lon", axis=0, tiled=False)
    own_weight = lax.dynamic_slice_in_dim(weight, lon * own_half, own_half, 2)
    own_weight = jnp.pad(own_weight, ((0, 0), (0, 0), (0, LANES - own_half)))
    own_weight = own_weight.reshape(groups, channels, basis * LANES)
    turned = quad_tiles.transpose(0, 1, 4, 2, 3).reshape(rows, entries * BLOCK, basis * BLOCK)
    live = jnp.arange(entries, dtype=jnp.int32)[None, :] < block_count[:, None]
    target = jnp.where(live, col_rows - (lat - HALO_DEV) * rows, window)
    far, near = quadrature(
        own_half, target, col_shift, lon[None].astype(jnp.int32), whole_out, own_weight, turned, window
    )

    same = near[0]
    other = lax.ppermute(near[1], "lon", [(0, 1), (1, 0)])
    offsets = [step for step in range(-HALO_DEV, HALO_DEV + 1) if step != 0]
    for at, offset in enumerate(offsets):
        reach = [
            (source, source + offset)
            for source in range(lat_devices)
            if 0 <= source + offset < lat_devices
        ]
        same = same + lax.ppermute(far[at, 0], "lat", reach)
        other = other + lax.ppermute(
            far[at, 1],
            ("lat", "lon"),
            [(2 * a + c, 2 * b + 1 - c) for a, b in reach for c in range(2)],
        )
    first = jnp.where(lon == 0, same, other)
    second = jnp.where(lon == 0, other, same)
    grad_input = jnp.concatenate([first, second], axis=1).transpose(1, 0, 2)
    return (grad_input, grad_weight)


def solution(mesh):
    in_specs = (
        P("ch", ("grp", "lat"), "lon"),
        P(None, "ch", ("grp", "lat"), "lon"),
        P(None, None, "ch"),
        P("lat", None, None, None, None),
        P("lat", None),
        P("lat", None),
        P("lat"),
    )
    out_specs = (P("ch", ("grp", "lat"), "lon"), P(("grp", "lat", "lon"), None, "ch"))
    return jax.shard_map(body, mesh=mesh, in_specs=in_specs, out_specs=out_specs, check_vma=False)
```

```python
import functools

import jax
import jax.numpy as jnp
from jax import lax
from jax.experimental import pallas as pl
from jax.experimental.pallas import tpu as pltpu
from jax.sharding import PartitionSpec as P

HALO_DEV = 2
BLOCK = 64
LANES = 128


MESH = pl.DeviceIdType.MESH
ROOM = 48 * 1024 * 1024


def gather_kernel(own_half, g_ref, q_hbm, k_hbm, whole, t_ref, w_ref, q_ref, k_ref, fetch, out_sem, in_sem):
    groups = lax.axis_size("ch")
    ch, lon = lax.axis_index("ch"), lax.axis_index("lon")
    rows, entries, basis = q_ref.shape[0], q_ref.shape[1], q_ref.shape[2]
    channels = g_ref.shape[1]
    tiles = pltpu.make_async_copy(q_hbm, q_ref, fetch.at[0])
    filters = pltpu.make_async_copy(k_hbm, k_ref, fetch.at[1])
    tiles.start()
    filters.start()
    barrier = pltpu.get_barrier_semaphore()
    for step in range(1, groups):
        pl.semaphore_signal(
            barrier, inc=1, device_id={"ch": lax.rem(ch + step, groups)}, device_id_type=MESH
        )
    pl.semaphore_signal(barrier, inc=1, device_id={"lon": 1 - lon}, device_id_type=MESH)
    pl.semaphore_wait(barrier, groups)

    across = [
        pltpu.make_async_remote_copy(
            src_ref=g_ref,
            dst_ref=whole.at[0, ch],
            send_sem=out_sem.at[step],
            recv_sem=in_sem.at[step],
            device_id={"ch": lax.rem(ch + step, groups)},
            device_id_type=MESH,
        )
        for step in range(1, groups)
    ]
    for copy in across:
        copy.start()

    def beside(step):
        source = lax.rem(ch + groups - step, groups)
        return pltpu.make_async_remote_copy(
            src_ref=g_ref if step == 0 else whole.at[0, source],
            dst_ref=whole.at[1, source],
            send_sem=out_sem.at[groups + step],
            recv_sem=in_sem.at[groups + step],
            device_id={"lon": 1 - lon},
            device_id_type=MESH,
        )

    forward = [beside(step) for step in range(groups)]
    forward[0].start()
    whole[0, ch] = g_ref[...]

    tiles.wait()
    for row in range(rows):

        @pl.loop(0, entries // 2)
        def _(pair):
            two = jnp.concatenate(
                [
                    q_ref[row, 2 * pair].reshape(basis * BLOCK, BLOCK),
                    q_ref[row, 2 * pair + 1].reshape(basis * BLOCK, BLOCK),
                ],
                axis=1,
            )
            t_ref[row, pl.ds(pl.multiple_of(pair * 2 * BLOCK, 2 * BLOCK), 2 * BLOCK)] = two.T

    filters.wait()
    w_ref[...] = jnp.zeros_like(w_ref)
    for half in range(2):

        @pl.when(lon == half)
        def _():
            for k in range(basis):
                for group in range(groups):
                    w_ref[group, :, k * LANES : k * LANES + own_half] = k_ref[
                        k,
                        group * channels : (group + 1) * channels,
                        half * own_half : (half + 1) * own_half,
                    ]

    for step in range(1, groups):
        across[step - 1].wait_recv()
        forward[step].start()
    for copy in across:
        copy.wait_send()
    for copy in forward:
        copy.wait()


def gathered(own_half, turned_out, quad_tiles, weight):
    rows, channels, width = turned_out.shape
    entries, basis = quad_tiles.shape[1:3]
    groups = lax.axis_size("ch")
    vmem = pl.BlockSpec(memory_space=pltpu.VMEM)
    far = pl.BlockSpec(memory_space=pl.ANY)
    return pl.pallas_call(
        functools.partial(gather_kernel, own_half),
        out_shape=(
            jax.ShapeDtypeStruct((2, groups, rows, channels, width), jnp.bfloat16),
            jax.ShapeDtypeStruct((rows, entries * BLOCK, basis * BLOCK), jnp.bfloat16),
            jax.ShapeDtypeStruct((groups, channels, basis * LANES), jnp.bfloat16),
        ),
        in_specs=[vmem, far, far],
        out_specs=(vmem, vmem, vmem),
        scratch_shapes=[
            pltpu.VMEM(quad_tiles.shape, jnp.bfloat16),
            pltpu.VMEM(weight.shape, jnp.bfloat16),
            pltpu.SemaphoreType.DMA((2,)),
            pltpu.SemaphoreType.DMA((2 * groups,)),
            pltpu.SemaphoreType.DMA((2 * groups,)),
        ],
        compiler_params=pltpu.CompilerParams(
            collective_id=0, has_side_effects=True, vmem_limit_bytes=ROOM
        ),
        cost_estimate=pl.CostEstimate(flops=0, bytes_accessed=10 * 2**20, transcendentals=0),
    )(turned_out, quad_tiles, weight)


def sum_kernel(far_ref, near_ref, out_ref, arrived, beside, out_sem, in_sem, pair_sem):
    lat_devices = lax.axis_size("lat")
    lat, lon = lax.axis_index("lat"), lax.axis_index("lon")
    own_half = near_ref.shape[2]
    offsets = [step for step in range(-HALO_DEV, HALO_DEV + 1) if step != 0]
    order = sorted(range(len(offsets)), key=lambda at: abs(offsets[at]))

    def reaches(step):
        return jnp.logical_and(lat + step >= 0, lat + step < lat_devices)

    barrier = pltpu.get_barrier_semaphore()
    pl.semaphore_signal(barrier, inc=1, device_id={"lon": 1 - lon}, device_id_type=MESH)
    for step in offsets:

        @pl.when(reaches(step))
        def _():
            for side in range(2):
                pl.semaphore_signal(
                    barrier,
                    inc=1,
                    device_id={"lat": lat + step, "lon": lax.rem(lon + side, 2)},
                    device_id_type=MESH,
                )

    pl.semaphore_wait(barrier, 1 + sum(jnp.where(reaches(step), 2, 0) for step in offsets))

    def message(at, side):
        return pltpu.make_async_remote_copy(
            src_ref=far_ref.at[at, side],
            dst_ref=arrived.at[at, side],
            send_sem=out_sem.at[at, side],
            recv_sem=in_sem.at[at, side],
            device_id={"lat": lat + offsets[at], "lon": lax.rem(lon + side, 2)},
            device_id_type=MESH,
        )

    pair = pltpu.make_async_remote_copy(
        src_ref=near_ref.at[1],
        dst_ref=beside,
        send_sem=pair_sem.at[0],
        recv_sem=pair_sem.at[1],
        device_id={"lon": 1 - lon},
        device_id_type=MESH,
    )
    for at in order:

        @pl.when(reaches(offsets[at]))
        def _():
            for side in range(2):
                message(at, side).start()

    pair.start()
    spans = [
        pl.ds(pl.multiple_of(lax.rem(lon + side, 2) * own_half, 8), own_half) for side in range(2)
    ]
    out_ref[:, spans[0]] = near_ref[0]
    pair.wait_recv()
    out_ref[:, spans[1]] = beside[...]
    for at in order:

        @pl.when(reaches(-offsets[at]))
        def _():
            for side in range(2):
                message(at, side).wait_recv()
                out_ref[:, spans[side]] += arrived[at, side].astype(jnp.float32)

    pair.wait_send()
    for at in order:

        @pl.when(reaches(offsets[at]))
        def _():
            for side in range(2):
                message(at, side).wait_send()


def summed(far, near):
    _, rows, own_half, width = near.shape
    vmem = pl.BlockSpec(memory_space=pltpu.VMEM)
    return pl.pallas_call(
        sum_kernel,
        out_shape=jax.ShapeDtypeStruct((rows, 2 * own_half, width), jnp.float32),
        in_specs=[vmem, vmem],
        out_specs=vmem,
        scratch_shapes=[
            pltpu.VMEM(far.shape, jnp.bfloat16),
            pltpu.VMEM(near.shape[1:], jnp.float32),
            pltpu.SemaphoreType.DMA(far.shape[:2]),
            pltpu.SemaphoreType.DMA(far.shape[:2]),
            pltpu.SemaphoreType.DMA((2,)),
        ],
        compiler_params=pltpu.CompilerParams(
            collective_id=1, has_side_effects=True, vmem_limit_bytes=ROOM
        ),
        cost_estimate=pl.CostEstimate(flops=0, bytes_accessed=40 * 2**20, transcendentals=0),
    )(far, near)


def quadrature_kernel(
    own_half, target, shift, lon, g_ref, w_ref, t_ref, far_ref, near_ref, acc, mixed, piece
):
    lon_halves, groups, rows, _, width = g_ref.shape
    window, cycle_blocks = acc.shape[0] - 1, acc.shape[1]
    entries = target.shape[1]
    basis = w_ref.shape[2] // LANES
    blocks = width // BLOCK
    pairs = cycle_blocks // 2
    acc[...] = jnp.zeros_like(acc)
    for row in range(rows):
        for half in range(lon_halves):
            total = None
            for group in range(groups):
                term = lax.dot_general(
                    g_ref[half, group, row],
                    w_ref[group],
                    (((0,), (0,)), ((), ())),
                    preferred_element_type=jnp.float32,
                )
                total = term if total is None else total + term
            total = total.astype(jnp.bfloat16)
            first = lax.rem(lon[0] + half, 2) * (blocks // 2)
            for block in range(blocks):
                for k in range(basis):
                    mixed[
                        first + block // 2,
                        k * BLOCK : (k + 1) * BLOCK,
                        (block % 2) * LANES : (block % 2 + 1) * LANES,
                    ] = total[block * BLOCK : (block + 1) * BLOCK, k * LANES : (k + 1) * LANES]

        @pl.loop(0, pairs)
        def _(pair):
            piece[...] = jnp.dot(
                t_ref[row], mixed[pair], preferred_element_type=jnp.float32
            )
            for entry in range(entries):
                for side in range(2):
                    place = lax.rem(2 * pair + side + shift[row, entry], cycle_blocks)
                    acc[target[row, entry], place] += piece[
                        entry * BLOCK : (entry + 1) * BLOCK, side * LANES : (side + 1) * LANES
                    ]

    mid = window // rows // 2
    for at in range(window):
        step, row = at // rows, at % rows
        for side in range(2):
            half = lax.rem(lon[0] + side, 2)
            turned = acc[at, pl.ds(half * blocks, blocks)].reshape(width, LANES).T[:own_half]
            if step == mid:
                near_ref[side, row] = turned
            else:
                far_ref[step - (step > mid), side, row] = turned.astype(jnp.bfloat16)


def quadrature(own_half, target, shift, lon, g, w, t, window):
    lon_halves, groups, rows, _, width = g.shape
    cycle_blocks = lon_halves * width // BLOCK
    depth = t.shape[2]
    vmem = pl.BlockSpec(memory_space=pltpu.VMEM)
    smem = pl.BlockSpec(memory_space=pltpu.SMEM)
    return pl.pallas_call(
        functools.partial(quadrature_kernel, own_half),
        out_shape=(
            jax.ShapeDtypeStruct(
                (window // rows - 1, 2, rows, own_half, width), jnp.bfloat16
            ),
            jax.ShapeDtypeStruct((2, rows, own_half, width), jnp.float32),
        ),
        in_specs=[smem, smem, smem, vmem, vmem, vmem],
        out_specs=(vmem, vmem),
        scratch_shapes=[
            pltpu.VMEM((window + 1, cycle_blocks, BLOCK, LANES), jnp.float32),
            pltpu.VMEM((cycle_blocks // 2, depth, 2 * LANES), jnp.bfloat16),
            pltpu.VMEM((t.shape[1], 2 * LANES), jnp.float32),
        ],
        compiler_params=pltpu.CompilerParams(vmem_limit_bytes=ROOM),
        cost_estimate=pl.CostEstimate(
            flops=9 * 10**9, bytes_accessed=10 * 2**20, transcendentals=0
        ),
    )(target, shift, lon, g, w, t)


def filter_gradient(full_out, saved_basis):
    product = jnp.einsum(
        "crow,kirw->coki", full_out, saved_basis, preferred_element_type=jnp.float32
    )
    groups, per, basis, channels = product.shape
    lat_devices = lax.axis_size("lat")
    lon_devices = lax.axis_size("lon")
    own_rows = groups * per // (lat_devices * lon_devices)
    if lat_devices > 8 or lon_devices != 2:
        return lax.psum_scatter(
            product.reshape(groups * per, basis, channels),
            ("lat", "lon"),
            scatter_dimension=0,
            tiled=True,
        )
    lat = lax.axis_index("lat")
    lon = lax.axis_index("lon")
    product = product.reshape(lat_devices, 2, own_rows, basis, channels)
    kept = lax.dynamic_index_in_dim(product, lon, 1, keepdims=False)
    given = lax.dynamic_index_in_dim(product, 1 - lon, 1, keepdims=False)
    kept = kept + lax.ppermute(given.astype(jnp.bfloat16), "lon", [(0, 1), (1, 0)])
    result = lax.dynamic_index_in_dim(kept, lat, 0, keepdims=False)
    narrow = kept.astype(jnp.bfloat16)
    for step in range(1, lat_devices):
        sent = lax.dynamic_index_in_dim(
            narrow, lax.rem(lat + step, lat_devices), 0, keepdims=False
        )
        result = result + lax.ppermute(
            sent, "lat", [(at, (at + step) % lat_devices) for at in range(lat_devices)]
        )
    return result


def body(grad_out, saved_basis, weight, quad_tiles, col_rows, col_shift, block_count):
    channels, rows, width = grad_out.shape
    entries = quad_tiles.shape[1]
    lat = lax.axis_index("lat")
    lon = lax.axis_index("lon")
    own_half = channels // 2
    window = (2 * HALO_DEV + 1) * rows

    whole_out, turned, own_weight = gathered(
        own_half, grad_out.transpose(1, 0, 2), quad_tiles, weight.transpose(1, 0, 2)
    )
    grad_weight = filter_gradient(whole_out[0], saved_basis)
    live = jnp.arange(entries, dtype=jnp.int32)[None, :] < block_count[:, None]
    target = jnp.where(live, col_rows - (lat - HALO_DEV) * rows, window)
    far, near = quadrature(
        own_half, target, col_shift, lon[None].astype(jnp.int32), whole_out, own_weight, turned, window
    )

    grad_input = summed(far, near).transpose(1, 0, 2)
    return (grad_input, grad_weight)


def solution(mesh):
    in_specs = (
        P("ch", ("grp", "lat"), "lon"),
        P(None, "ch", ("grp", "lat"), "lon"),
        P(None, None, "ch"),
        P("lat", None, None, None, None),
        P("lat", None),
        P("lat", None),
        P("lat"),
    )
    out_specs = (P("ch", ("grp", "lat"), "lon"), P(("grp", "lat", "lon"), None, "ch"))
    return jax.shard_map(body, mesh=mesh, in_specs=in_specs, out_specs=out_specs, check_vma=False)
```

```python
import functools

import jax
import jax.numpy as jnp
from jax import lax
from jax.experimental import pallas as pl
from jax.experimental.pallas import tpu as pltpu
from jax.sharding import PartitionSpec as P

HALO_DEV = 2
BLOCK = 64
LANES = 128


MESH = pl.DeviceIdType.MESH
ROOM = 48 * 1024 * 1024


def gather_kernel(g_ref, q_hbm, whole, t_ref, q_ref, fetch, out_sem, in_sem):
    groups = lax.axis_size("ch")
    ch, lon = lax.axis_index("ch"), lax.axis_index("lon")
    rows, entries, basis = q_ref.shape[0], q_ref.shape[1], q_ref.shape[2]
    tiles = pltpu.make_async_copy(q_hbm, q_ref, fetch.at[0])
    tiles.start()
    barrier = pltpu.get_barrier_semaphore()
    for step in range(1, groups):
        pl.semaphore_signal(
            barrier, inc=1, device_id={"ch": lax.rem(ch + step, groups)}, device_id_type=MESH
        )
    pl.semaphore_signal(barrier, inc=1, device_id={"lon": 1 - lon}, device_id_type=MESH)
    pl.semaphore_wait(barrier, groups)

    across = [
        pltpu.make_async_remote_copy(
            src_ref=g_ref,
            dst_ref=whole.at[0, ch],
            send_sem=out_sem.at[step],
            recv_sem=in_sem.at[step],
            device_id={"ch": lax.rem(ch + step, groups)},
            device_id_type=MESH,
        )
        for step in range(1, groups)
    ]
    for copy in across:
        copy.start()

    def beside(step):
        source = lax.rem(ch + groups - step, groups)
        return pltpu.make_async_remote_copy(
            src_ref=g_ref if step == 0 else whole.at[0, source],
            dst_ref=whole.at[1, source],
            send_sem=out_sem.at[groups + step],
            recv_sem=in_sem.at[groups + step],
            device_id={"lon": 1 - lon},
            device_id_type=MESH,
        )

    forward = [beside(step) for step in range(groups)]
    forward[0].start()
    whole[0, ch] = g_ref[...]

    tiles.wait()
    for row in range(rows):

        @pl.loop(0, entries // 2)
        def _(pair):
            two = jnp.concatenate(
                [
                    q_ref[row, 2 * pair].reshape(basis * BLOCK, BLOCK),
                    q_ref[row, 2 * pair + 1].reshape(basis * BLOCK, BLOCK),
                ],
                axis=1,
            )
            t_ref[row, pl.ds(pl.multiple_of(pair * 2 * BLOCK, 2 * BLOCK), 2 * BLOCK)] = two.T

    for step in range(1, groups):
        across[step - 1].wait_recv()
        forward[step].start()
    for copy in across:
        copy.wait_send()
    for copy in forward:
        copy.wait()


def gathered(turned_out, quad_tiles):
    rows, channels, width = turned_out.shape
    entries, basis = quad_tiles.shape[1:3]
    groups = lax.axis_size("ch")
    vmem = pl.BlockSpec(memory_space=pltpu.VMEM)
    far = pl.BlockSpec(memory_space=pl.ANY)
    return pl.pallas_call(
        gather_kernel,
        out_shape=(
            jax.ShapeDtypeStruct((2, groups, rows, channels, width), jnp.bfloat16),
            jax.ShapeDtypeStruct((rows, entries * BLOCK, basis * BLOCK), jnp.bfloat16),
        ),
        in_specs=[vmem, far],
        out_specs=(vmem, vmem),
        scratch_shapes=[
            pltpu.VMEM(quad_tiles.shape, jnp.bfloat16),
            pltpu.SemaphoreType.DMA((1,)),
            pltpu.SemaphoreType.DMA((2 * groups,)),
            pltpu.SemaphoreType.DMA((2 * groups,)),
        ],
        compiler_params=pltpu.CompilerParams(
            collective_id=0, has_side_effects=True, vmem_limit_bytes=ROOM
        ),
        cost_estimate=pl.CostEstimate(flops=0, bytes_accessed=10 * 2**20, transcendentals=0),
    )(turned_out, quad_tiles)


def sum_kernel(
    far_hbm, near_hbm, out_ref, own, relay, arrived, near, beside, fetch, relay_sem, row_sem, pair_sem
):
    lat_devices = lax.axis_size("lat")
    lat, lon = lax.axis_index("lat"), lax.axis_index("lon")
    rows, own_half = near.shape[:2]
    offsets = [step for step in range(-HALO_DEV, HALO_DEV + 1) if step != 0]
    ways = (1, -1)
    parts = [(way, side, row) for side in range(2) for row in range(rows) for way in range(2)]

    def reaches(step):
        return jnp.logical_and(lat + step >= 0, lat + step < lat_devices)

    loads = [pltpu.make_async_copy(near_hbm.at[0], near, fetch.at[2])]
    for way, step in enumerate(ways):
        loads.append(
            pltpu.make_async_copy(far_hbm.at[offsets.index(step)], own.at[way], fetch.at[way])
        )
    for load in loads:
        load.start()

    barrier = pltpu.get_barrier_semaphore()
    pl.semaphore_signal(barrier, inc=1, device_id={"lon": 1 - lon}, device_id_type=MESH)
    for step in ways:

        @pl.when(reaches(step))
        def _():
            for side in range(2):
                pl.semaphore_signal(
                    barrier,
                    inc=1,
                    device_id={"lat": lat + step, "lon": lax.rem(lon + side, 2)},
                    device_id_type=MESH,
                )

    pl.semaphore_wait(barrier, 1 + sum(jnp.where(reaches(step), 2, 0) for step in ways))

    def passed(way, side, row):
        return pltpu.make_async_remote_copy(
            src_ref=far_hbm.at[offsets.index(2 * ways[way]), side, row],
            dst_ref=relay.at[way, side, row],
            send_sem=relay_sem.at[0, way, side, row],
            recv_sem=relay_sem.at[1, way, side, row],
            device_id={"lat": lat + ways[way]},
            device_id_type=MESH,
        )

    def message(way, side, row):
        return pltpu.make_async_remote_copy(
            src_ref=own.at[way, side, row],
            dst_ref=arrived.at[way, side, row],
            send_sem=row_sem.at[0, way, side, row],
            recv_sem=row_sem.at[1, way, side, row],
            device_id={"lat": lat + ways[way], "lon": lax.rem(lon + side, 2)},
            device_id_type=MESH,
        )

    pair = pltpu.make_async_remote_copy(
        src_ref=near_hbm.at[1],
        dst_ref=beside,
        send_sem=pair_sem.at[0],
        recv_sem=pair_sem.at[1],
        device_id={"lon": 1 - lon},
        device_id_type=MESH,
    )
    for part in parts:

        @pl.when(reaches(2 * ways[part[0]]))
        def _():
            passed(*part).start()

    pair.start()
    spans = [
        pl.ds(pl.multiple_of(lax.rem(lon + side, 2) * own_half, 8), own_half) for side in range(2)
    ]
    for load in loads:
        load.wait()
    out_ref[:, spans[0]] = near[...]
    for part in parts:
        step = ways[part[0]]

        @pl.when(jnp.logical_and(reaches(step), reaches(-step)))
        def _():
            passed(*part).wait_recv()
            total = own[part].astype(jnp.float32) + relay[part].astype(jnp.float32)
            own[part] = total.astype(jnp.bfloat16)

        @pl.when(reaches(step))
        def _():
            message(*part).start()

    pair.wait_recv()
    out_ref[:, spans[1]] = beside[...]
    for part in parts:

        @pl.when(reaches(-ways[part[0]]))
        def _():
            message(*part).wait_recv()
            out_ref[part[2], spans[part[1]]] += arrived[part].astype(jnp.float32)

    pair.wait_send()
    for part in parts:
        step = ways[part[0]]

        @pl.when(reaches(2 * step))
        def _():
            passed(*part).wait_send()

        @pl.when(reaches(step))
        def _():
            message(*part).wait_send()


def summed(far, near):
    _, rows, own_half, width = near.shape
    either = pl.BlockSpec(memory_space=pl.ANY)
    return pl.pallas_call(
        sum_kernel,
        out_shape=jax.ShapeDtypeStruct((rows, 2 * own_half, width), jnp.float32),
        in_specs=[either, either],
        out_specs=pl.BlockSpec(memory_space=pltpu.VMEM),
        scratch_shapes=[
            *[pltpu.VMEM((2, 2, rows, own_half, width), jnp.bfloat16)] * 3,
            *[pltpu.VMEM((rows, own_half, width), jnp.float32)] * 2,
            pltpu.SemaphoreType.DMA((3,)),
            pltpu.SemaphoreType.DMA((2, 2, 2, rows)),
            pltpu.SemaphoreType.DMA((2, 2, 2, rows)),
            pltpu.SemaphoreType.DMA((2,)),
        ],
        compiler_params=pltpu.CompilerParams(
            collective_id=1, has_side_effects=True, vmem_limit_bytes=ROOM
        ),
        cost_estimate=pl.CostEstimate(flops=0, bytes_accessed=40 * 2**20, transcendentals=0),
    )(far, near)


def quadrature_kernel(
    own_half,
    target,
    shift,
    lon,
    g_ref,
    k_ref,
    t_ref,
    far_hbm,
    near_hbm,
    far_ref,
    near_ref,
    w_ref,
    acc,
    mixed,
    piece,
    store,
):
    lon_halves, groups, rows, channels, width = g_ref.shape
    window, cycle_blocks = acc.shape[0] - 1, acc.shape[1]
    entries = target.shape[1]
    basis = k_ref.shape[0]
    blocks = width // BLOCK
    pairs = cycle_blocks // 2
    acc[...] = jnp.zeros_like(acc)
    w_ref[...] = jnp.zeros_like(w_ref)
    for half in range(2):

        @pl.when(lon[0] == half)
        def _():
            for k in range(basis):
                for group in range(groups):
                    w_ref[group, :, k * LANES : k * LANES + own_half] = k_ref[
                        k,
                        group * channels : (group + 1) * channels,
                        half * own_half : (half + 1) * own_half,
                    ]

    for row in range(rows):
        for half in range(lon_halves):
            total = None
            for group in range(groups):
                term = lax.dot_general(
                    g_ref[half, group, row],
                    w_ref[group],
                    (((0,), (0,)), ((), ())),
                    preferred_element_type=jnp.float32,
                )
                total = term if total is None else total + term
            total = total.astype(jnp.bfloat16)
            first = lax.rem(lon[0] + half, 2) * (blocks // 2)
            for block in range(blocks):
                for k in range(basis):
                    mixed[
                        first + block // 2,
                        k * BLOCK : (k + 1) * BLOCK,
                        (block % 2) * LANES : (block % 2 + 1) * LANES,
                    ] = total[block * BLOCK : (block + 1) * BLOCK, k * LANES : (k + 1) * LANES]

        @pl.loop(0, pairs)
        def _(pair):
            piece[...] = jnp.dot(
                t_ref[row], mixed[pair], preferred_element_type=jnp.float32
            )
            for entry in range(entries):
                for side in range(2):
                    place = lax.rem(2 * pair + side + shift[row, entry], cycle_blocks)
                    acc[target[row, entry], place] += piece[
                        entry * BLOCK : (entry + 1) * BLOCK, side * LANES : (side + 1) * LANES
                    ]

    steps = window // rows
    mid = steps // 2
    saves = []
    for step in sorted(range(steps), key=lambda at: -abs(at - mid)):
        far = step - (step > mid)
        for side in range(2):
            half = lax.rem(lon[0] + side, 2)
            for row in range(rows):
                block = acc[step * rows + row, pl.ds(half * blocks, blocks)]
                turned = block.reshape(width, LANES).T[:own_half]
                if step == mid:
                    near_ref[side, row] = turned
                else:
                    far_ref[far, side, row] = turned.astype(jnp.bfloat16)
            if step == mid:
                save = pltpu.make_async_copy(near_ref.at[side], near_hbm.at[side], store.at[step, side])
            else:
                save = pltpu.make_async_copy(
                    far_ref.at[far, side], far_hbm.at[far, side], store.at[step, side]
                )
            save.start()
            saves.append(save)
    for save in saves:
        save.wait()


def quadrature(own_half, target, shift, lon, g, w, t, window):
    lon_halves, groups, rows, channels, width = g.shape
    cycle_blocks = lon_halves * width // BLOCK
    depth = t.shape[2]
    vmem = pl.BlockSpec(memory_space=pltpu.VMEM)
    smem = pl.BlockSpec(memory_space=pltpu.SMEM)
    return pl.pallas_call(
        functools.partial(quadrature_kernel, own_half),
        out_shape=(
            jax.ShapeDtypeStruct(
                (window // rows - 1, 2, rows, own_half, width), jnp.bfloat16
            ),
            jax.ShapeDtypeStruct((2, rows, own_half, width), jnp.float32),
        ),
        in_specs=[smem, smem, smem, vmem, vmem, vmem],
        out_specs=(pl.BlockSpec(memory_space=pl.ANY), pl.BlockSpec(memory_space=pl.ANY)),
        scratch_shapes=[
            pltpu.VMEM((window // rows - 1, 2, rows, own_half, width), jnp.bfloat16),
            pltpu.VMEM((2, rows, own_half, width), jnp.float32),
            pltpu.VMEM((groups, channels, w.shape[0] * LANES), jnp.bfloat16),
            pltpu.VMEM((window + 1, cycle_blocks, BLOCK, LANES), jnp.float32),
            pltpu.VMEM((cycle_blocks // 2, depth, 2 * LANES), jnp.bfloat16),
            pltpu.VMEM((t.shape[1], 2 * LANES), jnp.float32),
            pltpu.SemaphoreType.DMA((window // rows, 2)),
        ],
        compiler_params=pltpu.CompilerParams(vmem_limit_bytes=ROOM),
        cost_estimate=pl.CostEstimate(
            flops=9 * 10**9, bytes_accessed=10 * 2**20, transcendentals=0
        ),
    )(target, shift, lon, g, w, t)


def filter_gradient(full_out, saved_basis):
    groups, rows, channels, width = full_out.shape
    basis = saved_basis.shape[0]
    lat_devices = lax.axis_size("lat")
    lon_devices = lax.axis_size("lon")
    own_rows = groups * channels // (lat_devices * lon_devices)
    if lat_devices > 8 or lon_devices != 2 or channels % (2 * own_rows):
        product = jnp.einsum(
            "crow,kirw->coki", full_out, saved_basis, preferred_element_type=jnp.float32
        )
        return lax.psum_scatter(
            product.reshape(groups * channels, basis, channels),
            ("lat", "lon"),
            scatter_dimension=0,
            tiled=True,
        )
    lat = lax.axis_index("lat")
    lon = lax.axis_index("lon")
    split = full_out.reshape(groups, rows, channels // (2 * own_rows), 2, own_rows, width)

    def half(which):
        product = jnp.einsum(
            "crlow,kirw->cloki",
            lax.dynamic_index_in_dim(split, which, 3, keepdims=False),
            saved_basis,
            preferred_element_type=jnp.float32,
        )
        return product.reshape(lat_devices, own_rows, basis, channels)

    received = lax.ppermute(half(1 - lon).astype(jnp.bfloat16), "lon", [(0, 1), (1, 0)])
    kept = half(lon)

    def both(step):
        at = lax.rem(lat + step, lat_devices)
        mine = lax.dynamic_index_in_dim(kept, at, 0, keepdims=False)
        return mine + lax.dynamic_index_in_dim(received, at, 0, keepdims=False)

    result = both(0)
    for step in range(1, lat_devices):
        result = result + lax.ppermute(
            both(step).astype(jnp.bfloat16),
            "lat",
            [(at, (at + step) % lat_devices) for at in range(lat_devices)],
        )
    return result


def body(grad_out, saved_basis, weight, quad_tiles, col_rows, col_shift, block_count):
    channels, rows, width = grad_out.shape
    entries = quad_tiles.shape[1]
    lat = lax.axis_index("lat")
    lon = lax.axis_index("lon")
    own_half = channels // 2
    window = (2 * HALO_DEV + 1) * rows

    whole_out, turned = gathered(grad_out.transpose(1, 0, 2), quad_tiles)
    grad_weight = filter_gradient(whole_out[0], saved_basis)
    live = jnp.arange(entries, dtype=jnp.int32)[None, :] < block_count[:, None]
    target = jnp.where(live, col_rows - (lat - HALO_DEV) * rows, window)
    far, near = quadrature(
        own_half, target, col_shift, lon[None].astype(jnp.int32), whole_out, weight.transpose(1, 0, 2), turned, window
    )

    grad_input = summed(far, near).transpose(1, 0, 2)
    return (grad_input, grad_weight)


def solution(mesh):
    in_specs = (
        P("ch", ("grp", "lat"), "lon"),
        P(None, "ch", ("grp", "lat"), "lon"),
        P(None, None, "ch"),
        P("lat", None, None, None, None),
        P("lat", None),
        P("lat", None),
        P("lat"),
    )
    out_specs = (P("ch", ("grp", "lat"), "lon"), P(("grp", "lat", "lon"), None, "ch"))
    return jax.shard_map(body, mesh=mesh, in_specs=in_specs, out_specs=out_specs, check_vma=False)
```

```python
import functools

import jax
import jax.numpy as jnp
from jax import lax
from jax.experimental import pallas as pl
from jax.experimental.pallas import tpu as pltpu
from jax.sharding import PartitionSpec as P

HALO_DEV = 2
BLOCK = 64
LANES = 128


MESH = pl.DeviceIdType.MESH
MIB = 1024 * 1024


def gather_kernel(g_ref, q_hbm, whole, t_ref, q_ref, fetch, out_sem, in_sem):
    groups = lax.axis_size("ch")
    ch, lon = lax.axis_index("ch"), lax.axis_index("lon")
    rows, entries, basis = q_ref.shape[0], q_ref.shape[1], q_ref.shape[2]
    tiles = pltpu.make_async_copy(q_hbm, q_ref, fetch.at[0])
    tiles.start()
    barrier = pltpu.get_barrier_semaphore()
    for step in range(1, groups):
        pl.semaphore_signal(
            barrier, inc=1, device_id={"ch": lax.rem(ch + step, groups)}, device_id_type=MESH
        )
    pl.semaphore_signal(barrier, inc=1, device_id={"lon": 1 - lon}, device_id_type=MESH)
    pl.semaphore_wait(barrier, groups)

    def across(step, row):
        return pltpu.make_async_remote_copy(
            src_ref=g_ref.at[row],
            dst_ref=whole.at[0, ch, row],
            send_sem=out_sem.at[step, row],
            recv_sem=in_sem.at[step, row],
            device_id={"ch": lax.rem(ch + step, groups)},
            device_id_type=MESH,
        )

    def beside(step, row):
        source = lax.rem(ch + groups - step, groups)
        return pltpu.make_async_remote_copy(
            src_ref=g_ref.at[row] if step == 0 else whole.at[0, source, row],
            dst_ref=whole.at[1, source, row],
            send_sem=out_sem.at[groups + step, row],
            recv_sem=in_sem.at[groups + step, row],
            device_id={"lon": 1 - lon},
            device_id_type=MESH,
        )

    for row in range(rows):
        for step in range(1, groups):
            across(step, row).start()
    for row in range(rows):
        beside(0, row).start()
    whole[0, ch] = g_ref[...]

    tiles.wait()
    for row in range(rows):

        @pl.loop(0, entries // 2)
        def _(pair):
            two = jnp.concatenate(
                [
                    q_ref[row, 2 * pair].reshape(basis * BLOCK, BLOCK),
                    q_ref[row, 2 * pair + 1].reshape(basis * BLOCK, BLOCK),
                ],
                axis=1,
            )
            t_ref[row, pl.ds(pl.multiple_of(pair * 2 * BLOCK, 2 * BLOCK), 2 * BLOCK)] = two.T

        for step in range(1, groups):
            across(step, row).wait_recv()
            beside(step, row).start()

    for row in range(rows):
        for step in range(1, groups):
            across(step, row).wait_send()
        for step in range(groups):
            beside(step, row).wait()


def gathered(turned_out, quad_tiles):
    rows, channels, width = turned_out.shape
    entries, basis = quad_tiles.shape[1:3]
    groups = lax.axis_size("ch")
    vmem = pl.BlockSpec(memory_space=pltpu.VMEM)
    far = pl.BlockSpec(memory_space=pl.ANY)
    return pl.pallas_call(
        gather_kernel,
        out_shape=(
            jax.ShapeDtypeStruct((2, groups, rows, channels, width), jnp.bfloat16),
            jax.ShapeDtypeStruct((rows, entries * BLOCK, basis * BLOCK), jnp.bfloat16),
        ),
        in_specs=[vmem, far],
        out_specs=(vmem, vmem),
        scratch_shapes=[
            pltpu.VMEM(quad_tiles.shape, jnp.bfloat16),
            pltpu.SemaphoreType.DMA((1,)),
            pltpu.SemaphoreType.DMA((2 * groups, rows)),
            pltpu.SemaphoreType.DMA((2 * groups, rows)),
        ],
        compiler_params=pltpu.CompilerParams(
            collective_id=0, has_side_effects=True, vmem_limit_bytes=20 * MIB
        ),
        cost_estimate=pl.CostEstimate(flops=0, bytes_accessed=10 * 2**20, transcendentals=0),
    )(turned_out, quad_tiles)


def sum_kernel(
    far_hbm, near_hbm, out_ref, own, relay, arrived, near, beside, fetch, relay_sem, row_sem, pair_sem
):
    lat_devices = lax.axis_size("lat")
    lat, lon = lax.axis_index("lat"), lax.axis_index("lon")
    rows, own_half = near.shape[:2]
    offsets = [step for step in range(-HALO_DEV, HALO_DEV + 1) if step != 0]
    ways = (1, -1)
    parts = [(way, side, row) for side in range(2) for row in range(rows) for way in range(2)]

    def reaches(step):
        return jnp.logical_and(lat + step >= 0, lat + step < lat_devices)

    loads = [pltpu.make_async_copy(near_hbm.at[0], near, fetch.at[2])]
    for way, step in enumerate(ways):
        loads.append(
            pltpu.make_async_copy(far_hbm.at[offsets.index(step)], own.at[way], fetch.at[way])
        )
    for load in loads:
        load.start()

    barrier = pltpu.get_barrier_semaphore()
    pl.semaphore_signal(barrier, inc=1, device_id={"lon": 1 - lon}, device_id_type=MESH)
    for step in ways:

        @pl.when(reaches(step))
        def _():
            for side in range(2):
                pl.semaphore_signal(
                    barrier,
                    inc=1,
                    device_id={"lat": lat + step, "lon": lax.rem(lon + side, 2)},
                    device_id_type=MESH,
                )

    pl.semaphore_wait(barrier, 1 + sum(jnp.where(reaches(step), 2, 0) for step in ways))

    def passed(way, side, row):
        return pltpu.make_async_remote_copy(
            src_ref=far_hbm.at[offsets.index(2 * ways[way]), side, row],
            dst_ref=relay.at[way, side, row],
            send_sem=relay_sem.at[0, way, side, row],
            recv_sem=relay_sem.at[1, way, side, row],
            device_id={"lat": lat + ways[way]},
            device_id_type=MESH,
        )

    def message(way, side, row):
        return pltpu.make_async_remote_copy(
            src_ref=own.at[way, side, row],
            dst_ref=arrived.at[way, side, row],
            send_sem=row_sem.at[0, way, side, row],
            recv_sem=row_sem.at[1, way, side, row],
            device_id={"lat": lat + ways[way], "lon": lax.rem(lon + side, 2)},
            device_id_type=MESH,
        )

    pair = pltpu.make_async_remote_copy(
        src_ref=near_hbm.at[1],
        dst_ref=beside,
        send_sem=pair_sem.at[0],
        recv_sem=pair_sem.at[1],
        device_id={"lon": 1 - lon},
        device_id_type=MESH,
    )
    for part in parts:

        @pl.when(reaches(2 * ways[part[0]]))
        def _():
            passed(*part).start()

    pair.start()
    spans = [
        pl.ds(pl.multiple_of(lax.rem(lon + side, 2) * own_half, 8), own_half) for side in range(2)
    ]
    for load in loads:
        load.wait()
    out_ref[:, spans[0]] = near[...]
    for part in parts:
        step = ways[part[0]]

        @pl.when(jnp.logical_and(reaches(step), reaches(-step)))
        def _():
            passed(*part).wait_recv()
            total = own[part].astype(jnp.float32) + relay[part].astype(jnp.float32)
            own[part] = total.astype(jnp.bfloat16)

        @pl.when(reaches(step))
        def _():
            message(*part).start()

    pair.wait_recv()
    out_ref[:, spans[1]] = beside[...]
    for part in parts:

        @pl.when(reaches(-ways[part[0]]))
        def _():
            message(*part).wait_recv()
            out_ref[part[2], spans[part[1]]] += arrived[part].astype(jnp.float32)

    pair.wait_send()
    for part in parts:
        step = ways[part[0]]

        @pl.when(reaches(2 * step))
        def _():
            passed(*part).wait_send()

        @pl.when(reaches(step))
        def _():
            message(*part).wait_send()


def summed(far, near):
    _, rows, own_half, width = near.shape
    either = pl.BlockSpec(memory_space=pl.ANY)
    return pl.pallas_call(
        sum_kernel,
        out_shape=jax.ShapeDtypeStruct((rows, 2 * own_half, width), jnp.float32),
        in_specs=[either, either],
        out_specs=pl.BlockSpec(memory_space=pltpu.VMEM),
        scratch_shapes=[
            *[pltpu.VMEM((2, 2, rows, own_half, width), jnp.bfloat16)] * 3,
            *[pltpu.VMEM((rows, own_half, width), jnp.float32)] * 2,
            pltpu.SemaphoreType.DMA((3,)),
            pltpu.SemaphoreType.DMA((2, 2, 2, rows)),
            pltpu.SemaphoreType.DMA((2, 2, 2, rows)),
            pltpu.SemaphoreType.DMA((2,)),
        ],
        compiler_params=pltpu.CompilerParams(
            collective_id=1, has_side_effects=True, vmem_limit_bytes=16 * MIB
        ),
        cost_estimate=pl.CostEstimate(flops=0, bytes_accessed=40 * 2**20, transcendentals=0),
    )(far, near)


def quadrature_kernel(
    own_half,
    target,
    shift,
    lon,
    g_ref,
    k_ref,
    t_ref,
    far_hbm,
    near_hbm,
    far_ref,
    near_ref,
    w_ref,
    acc,
    mixed,
    piece,
    store,
):
    lon_halves, groups, rows, channels, width = g_ref.shape
    window, cycle_blocks = acc.shape[0] - 1, acc.shape[1]
    entries = target.shape[1]
    basis = k_ref.shape[0]
    blocks = width // BLOCK
    pairs = cycle_blocks // 2
    acc[...] = jnp.zeros_like(acc)
    w_ref[...] = jnp.zeros_like(w_ref)
    for half in range(2):

        @pl.when(lon[0] == half)
        def _():
            for k in range(basis):
                for group in range(groups):
                    w_ref[group, :, k * LANES : k * LANES + own_half] = k_ref[
                        k,
                        group * channels : (group + 1) * channels,
                        half * own_half : (half + 1) * own_half,
                    ]

    for row in range(rows):
        for half in range(lon_halves):
            total = None
            for group in range(groups):
                term = lax.dot_general(
                    g_ref[half, group, row],
                    w_ref[group],
                    (((0,), (0,)), ((), ())),
                    preferred_element_type=jnp.float32,
                )
                total = term if total is None else total + term
            total = total.astype(jnp.bfloat16)
            first = lax.rem(lon[0] + half, 2) * (blocks // 2)
            for block in range(blocks):
                for k in range(basis):
                    mixed[
                        first + block // 2,
                        k * BLOCK : (k + 1) * BLOCK,
                        (block % 2) * LANES : (block % 2 + 1) * LANES,
                    ] = total[block * BLOCK : (block + 1) * BLOCK, k * LANES : (k + 1) * LANES]

        def multiply(pair, slot):
            piece[slot] = jnp.dot(t_ref[row], mixed[pair], preferred_element_type=jnp.float32)

        def put(pair, slot):
            for entry in range(entries):
                for side in range(2):
                    place = lax.rem(2 * pair + side + shift[row, entry], cycle_blocks)
                    acc[target[row, entry], place] += piece[
                        slot,
                        entry * BLOCK : (entry + 1) * BLOCK,
                        side * LANES : (side + 1) * LANES,
                    ]

        multiply(0, 0)

        @pl.loop(0, pairs // 2 - 1)
        def _(step):
            multiply(2 * step + 1, 1)
            put(2 * step, 0)
            multiply(2 * step + 2, 0)
            put(2 * step + 1, 1)

        multiply(pairs - 1, 1)
        put(pairs - 2, 0)
        put(pairs - 1, 1)

    steps = window // rows
    mid = steps // 2
    saves = []
    for step in sorted(range(steps), key=lambda at: -abs(at - mid)):
        far = step - (step > mid)
        for side in range(2):
            half = lax.rem(lon[0] + side, 2)
            for row in range(rows):
                block = acc[step * rows + row, pl.ds(half * blocks, blocks)]
                turned = block.reshape(width, LANES).T[:own_half]
                if step == mid:
                    near_ref[side, row] = turned
                else:
                    far_ref[far, side, row] = turned.astype(jnp.bfloat16)
            if step == mid:
                save = pltpu.make_async_copy(near_ref.at[side], near_hbm.at[side], store.at[step, side])
            else:
                save = pltpu.make_async_copy(
                    far_ref.at[far, side], far_hbm.at[far, side], store.at[step, side]
                )
            save.start()
            saves.append(save)
    for save in saves:
        save.wait()


def quadrature(own_half, target, shift, lon, g, w, t, window):
    lon_halves, groups, rows, channels, width = g.shape
    cycle_blocks = lon_halves * width // BLOCK
    depth = t.shape[2]
    vmem = pl.BlockSpec(memory_space=pltpu.VMEM)
    smem = pl.BlockSpec(memory_space=pltpu.SMEM)
    return pl.pallas_call(
        functools.partial(quadrature_kernel, own_half),
        out_shape=(
            jax.ShapeDtypeStruct(
                (window // rows - 1, 2, rows, own_half, width), jnp.bfloat16
            ),
            jax.ShapeDtypeStruct((2, rows, own_half, width), jnp.float32),
        ),
        in_specs=[smem, smem, smem, vmem, vmem, vmem],
        out_specs=(pl.BlockSpec(memory_space=pl.ANY), pl.BlockSpec(memory_space=pl.ANY)),
        scratch_shapes=[
            pltpu.VMEM((window // rows - 1, 2, rows, own_half, width), jnp.bfloat16),
            pltpu.VMEM((2, rows, own_half, width), jnp.float32),
            pltpu.VMEM((groups, channels, w.shape[0] * LANES), jnp.bfloat16),
            pltpu.VMEM((window + 1, cycle_blocks, BLOCK, LANES), jnp.float32),
            pltpu.VMEM((cycle_blocks // 2, depth, 2 * LANES), jnp.bfloat16),
            pltpu.VMEM((2, t.shape[1], 2 * LANES), jnp.float32),
            pltpu.SemaphoreType.DMA((window // rows, 2)),
        ],
        compiler_params=pltpu.CompilerParams(vmem_limit_bytes=36 * MIB),
        cost_estimate=pl.CostEstimate(
            flops=9 * 10**9, bytes_accessed=10 * 2**20, transcendentals=0
        ),
    )(target, shift, lon, g, w, t)


def filter_gradient(full_out, saved_basis):
    groups, rows, channels, width = full_out.shape
    basis = saved_basis.shape[0]
    lat_devices = lax.axis_size("lat")
    lon_devices = lax.axis_size("lon")
    own_rows = groups * channels // (lat_devices * lon_devices)
    if lat_devices > 8 or lon_devices != 2 or channels % (2 * own_rows):
        product = jnp.einsum(
            "crow,kirw->coki", full_out, saved_basis, preferred_element_type=jnp.float32
        )
        return lax.psum_scatter(
            product.reshape(groups * channels, basis, channels),
            ("lat", "lon"),
            scatter_dimension=0,
            tiled=True,
        )
    lat = lax.axis_index("lat")
    lon = lax.axis_index("lon")
    split = full_out.reshape(groups, rows, channels // (2 * own_rows), 2, own_rows, width)

    def half(which):
        product = jnp.einsum(
            "crlow,kirw->cloki",
            lax.dynamic_index_in_dim(split, which, 3, keepdims=False),
            saved_basis,
            preferred_element_type=jnp.float32,
        )
        return product.reshape(lat_devices, own_rows, basis, channels)

    received = lax.ppermute(half(1 - lon).astype(jnp.bfloat16), "lon", [(0, 1), (1, 0)])
    kept = half(lon)

    def both(step):
        at = lax.rem(lat + step, lat_devices)
        mine = lax.dynamic_index_in_dim(kept, at, 0, keepdims=False)
        return mine + lax.dynamic_index_in_dim(received, at, 0, keepdims=False)

    result = both(0)
    for step in range(1, lat_devices):
        result = result + lax.ppermute(
            both(step).astype(jnp.bfloat16),
            "lat",
            [(at, (at + step) % lat_devices) for at in range(lat_devices)],
        )
    return result


def body(grad_out, saved_basis, weight, quad_tiles, col_rows, col_shift, block_count):
    channels, rows, width = grad_out.shape
    entries = quad_tiles.shape[1]
    lat = lax.axis_index("lat")
    lon = lax.axis_index("lon")
    own_half = channels // 2
    window = (2 * HALO_DEV + 1) * rows

    whole_out, turned = gathered(grad_out.transpose(1, 0, 2), quad_tiles)
    grad_weight = filter_gradient(whole_out[0], saved_basis)
    live = jnp.arange(entries, dtype=jnp.int32)[None, :] < block_count[:, None]
    target = jnp.where(live, col_rows - (lat - HALO_DEV) * rows, window)
    far, near = quadrature(
        own_half, target, col_shift, lon[None].astype(jnp.int32), whole_out, weight.transpose(1, 0, 2), turned, window
    )

    grad_input = summed(far, near).transpose(1, 0, 2)
    return (grad_input, grad_weight)


def solution(mesh):
    in_specs = (
        P("ch", ("grp", "lat"), "lon"),
        P(None, "ch", ("grp", "lat"), "lon"),
        P(None, None, "ch"),
        P("lat", None, None, None, None),
        P("lat", None),
        P("lat", None),
        P("lat"),
    )
    out_specs = (P("ch", ("grp", "lat"), "lon"), P(("grp", "lat", "lon"), None, "ch"))
    return jax.shard_map(body, mesh=mesh, in_specs=in_specs, out_specs=out_specs, check_vma=False)
```

```python
import functools

import jax
import jax.numpy as jnp
from jax import lax
from jax.experimental import pallas as pl
from jax.experimental.pallas import tpu as pltpu
from jax.sharding import PartitionSpec as P

HALO_DEV = 2
BLOCK = 64
LANES = 128


MESH = pl.DeviceIdType.MESH
MIB = 1024 * 1024


def gather_kernel(g_ref, q_hbm, whole, t_ref, q_ref, fetch, out_sem, in_sem):
    groups = lax.axis_size("ch")
    ch, lon = lax.axis_index("ch"), lax.axis_index("lon")
    rows, entries, basis = q_ref.shape[0], q_ref.shape[1], q_ref.shape[2]
    tiles = pltpu.make_async_copy(q_hbm, q_ref, fetch.at[0])
    tiles.start()
    barrier = pltpu.get_barrier_semaphore()
    for step in range(1, groups):
        pl.semaphore_signal(
            barrier, inc=1, device_id={"ch": lax.rem(ch + step, groups)}, device_id_type=MESH
        )
    pl.semaphore_signal(barrier, inc=1, device_id={"lon": 1 - lon}, device_id_type=MESH)
    pl.semaphore_wait(barrier, groups)

    def across(step, row):
        return pltpu.make_async_remote_copy(
            src_ref=g_ref.at[row],
            dst_ref=whole.at[0, ch, row],
            send_sem=out_sem.at[step, row],
            recv_sem=in_sem.at[step, row],
            device_id={"ch": lax.rem(ch + step, groups)},
            device_id_type=MESH,
        )

    def beside(step, row):
        source = lax.rem(ch + groups - step, groups)
        return pltpu.make_async_remote_copy(
            src_ref=g_ref.at[row] if step == 0 else whole.at[0, source, row],
            dst_ref=whole.at[1, source, row],
            send_sem=out_sem.at[groups + step, row],
            recv_sem=in_sem.at[groups + step, row],
            device_id={"lon": 1 - lon},
            device_id_type=MESH,
        )

    for row in range(rows):
        for step in range(1, groups):
            across(step, row).start()
    for row in range(rows):
        beside(0, row).start()
    whole[0, ch] = g_ref[...]

    tiles.wait()
    for row in range(rows):

        @pl.loop(0, entries // 2)
        def _(pair):
            two = jnp.concatenate(
                [
                    q_ref[row, 2 * pair].reshape(basis * BLOCK, BLOCK),
                    q_ref[row, 2 * pair + 1].reshape(basis * BLOCK, BLOCK),
                ],
                axis=1,
            )
            t_ref[row, pl.ds(pl.multiple_of(pair * 2 * BLOCK, 2 * BLOCK), 2 * BLOCK)] = two.T

        for step in range(1, groups):
            across(step, row).wait_recv()
            beside(step, row).start()

    for row in range(rows):
        for step in range(1, groups):
            across(step, row).wait_send()
        for step in range(groups):
            beside(step, row).wait()


def gathered(turned_out, quad_tiles):
    rows, channels, width = turned_out.shape
    entries, basis = quad_tiles.shape[1:3]
    groups = lax.axis_size("ch")
    vmem = pl.BlockSpec(memory_space=pltpu.VMEM)
    far = pl.BlockSpec(memory_space=pl.ANY)
    return pl.pallas_call(
        gather_kernel,
        out_shape=(
            jax.ShapeDtypeStruct((2, groups, rows, channels, width), jnp.bfloat16),
            jax.ShapeDtypeStruct((rows, entries * BLOCK, basis * BLOCK), jnp.bfloat16),
        ),
        in_specs=[vmem, far],
        out_specs=(vmem, vmem),
        scratch_shapes=[
            pltpu.VMEM(quad_tiles.shape, jnp.bfloat16),
            pltpu.SemaphoreType.DMA((1,)),
            pltpu.SemaphoreType.DMA((2 * groups, rows)),
            pltpu.SemaphoreType.DMA((2 * groups, rows)),
        ],
        compiler_params=pltpu.CompilerParams(
            collective_id=0, has_side_effects=True, vmem_limit_bytes=48 * MIB
        ),
        cost_estimate=pl.CostEstimate(flops=0, bytes_accessed=10 * 2**20, transcendentals=0),
    )(turned_out, quad_tiles)


def sum_kernel(
    far_hbm, near_hbm, out_ref, own, relay, arrived, near, beside, fetch, relay_sem, row_sem, pair_sem
):
    lat_devices = lax.axis_size("lat")
    lat, lon = lax.axis_index("lat"), lax.axis_index("lon")
    rows, own_half = near.shape[:2]
    offsets = [step for step in range(-HALO_DEV, HALO_DEV + 1) if step != 0]
    ways = (1, -1)
    parts = [(way, side, row) for side in range(2) for row in range(rows) for way in range(2)]

    def reaches(step):
        return jnp.logical_and(lat + step >= 0, lat + step < lat_devices)

    loads = [pltpu.make_async_copy(near_hbm.at[0], near, fetch.at[2])]
    for way, step in enumerate(ways):
        loads.append(
            pltpu.make_async_copy(far_hbm.at[offsets.index(step)], own.at[way], fetch.at[way])
        )
    for load in loads:
        load.start()

    barrier = pltpu.get_barrier_semaphore()
    pl.semaphore_signal(barrier, inc=1, device_id={"lon": 1 - lon}, device_id_type=MESH)
    for step in ways:

        @pl.when(reaches(step))
        def _():
            for side in range(2):
                pl.semaphore_signal(
                    barrier,
                    inc=1,
                    device_id={"lat": lat + step, "lon": lax.rem(lon + side, 2)},
                    device_id_type=MESH,
                )

    pl.semaphore_wait(barrier, 1 + sum(jnp.where(reaches(step), 2, 0) for step in ways))

    def passed(way, side, row):
        return pltpu.make_async_remote_copy(
            src_ref=far_hbm.at[offsets.index(2 * ways[way]), side, row],
            dst_ref=relay.at[way, side, row],
            send_sem=relay_sem.at[0, way, side, row],
            recv_sem=relay_sem.at[1, way, side, row],
            device_id={"lat": lat + ways[way]},
            device_id_type=MESH,
        )

    def message(way, side, row):
        return pltpu.make_async_remote_copy(
            src_ref=own.at[way, side, row],
            dst_ref=arrived.at[way, side, row],
            send_sem=row_sem.at[0, way, side, row],
            recv_sem=row_sem.at[1, way, side, row],
            device_id={"lat": lat + ways[way], "lon": lax.rem(lon + side, 2)},
            device_id_type=MESH,
        )

    pair = pltpu.make_async_remote_copy(
        src_ref=near_hbm.at[1],
        dst_ref=beside,
        send_sem=pair_sem.at[0],
        recv_sem=pair_sem.at[1],
        device_id={"lon": 1 - lon},
        device_id_type=MESH,
    )
    for part in parts:

        @pl.when(reaches(2 * ways[part[0]]))
        def _():
            passed(*part).start()

    pair.start()
    spans = [
        pl.ds(pl.multiple_of(lax.rem(lon + side, 2) * own_half, 8), own_half) for side in range(2)
    ]
    for load in loads:
        load.wait()
    out_ref[:, spans[0]] = near[...]
    for part in parts:
        step = ways[part[0]]

        @pl.when(jnp.logical_and(reaches(step), reaches(-step)))
        def _():
            passed(*part).wait_recv()
            total = own[part].astype(jnp.float32) + relay[part].astype(jnp.float32)
            own[part] = total.astype(jnp.bfloat16)

        @pl.when(reaches(step))
        def _():
            message(*part).start()

    pair.wait_recv()
    out_ref[:, spans[1]] = beside[...]
    for part in parts:

        @pl.when(reaches(-ways[part[0]]))
        def _():
            message(*part).wait_recv()
            out_ref[part[2], spans[part[1]]] += arrived[part].astype(jnp.float32)

    pair.wait_send()
    for part in parts:
        step = ways[part[0]]

        @pl.when(reaches(2 * step))
        def _():
            passed(*part).wait_send()

        @pl.when(reaches(step))
        def _():
            message(*part).wait_send()


def summed(far, near):
    _, rows, own_half, width = near.shape
    either = pl.BlockSpec(memory_space=pl.ANY)
    return pl.pallas_call(
        sum_kernel,
        out_shape=jax.ShapeDtypeStruct((rows, 2 * own_half, width), jnp.float32),
        in_specs=[either, either],
        out_specs=pl.BlockSpec(memory_space=pltpu.VMEM),
        scratch_shapes=[
            *[pltpu.VMEM((2, 2, rows, own_half, width), jnp.bfloat16)] * 3,
            *[pltpu.VMEM((rows, own_half, width), jnp.float32)] * 2,
            pltpu.SemaphoreType.DMA((3,)),
            pltpu.SemaphoreType.DMA((2, 2, 2, rows)),
            pltpu.SemaphoreType.DMA((2, 2, 2, rows)),
            pltpu.SemaphoreType.DMA((2,)),
        ],
        compiler_params=pltpu.CompilerParams(
            collective_id=1, has_side_effects=True, vmem_limit_bytes=16 * MIB
        ),
        cost_estimate=pl.CostEstimate(flops=0, bytes_accessed=40 * 2**20, transcendentals=0),
    )(far, near)


def quadrature_kernel(
    own_half,
    target,
    shift,
    lon,
    g_ref,
    k_ref,
    t_ref,
    far_hbm,
    near_hbm,
    far_ref,
    near_ref,
    w_ref,
    acc,
    mixed,
    piece,
    store,
):
    lon_halves, groups, rows, channels, width = g_ref.shape
    window, cycle_blocks = acc.shape[0] - 1, acc.shape[1]
    entries = target.shape[1]
    basis = k_ref.shape[0]
    blocks = width // BLOCK
    pairs = cycle_blocks // 2
    acc[...] = jnp.zeros_like(acc)
    w_ref[...] = jnp.zeros_like(w_ref)
    for half in range(2):

        @pl.when(lon[0] == half)
        def _():
            for k in range(basis):
                for group in range(groups):
                    w_ref[group, :, k * LANES : k * LANES + own_half] = k_ref[
                        k,
                        group * channels : (group + 1) * channels,
                        half * own_half : (half + 1) * own_half,
                    ]

    for row in range(rows):
        for half in range(lon_halves):
            total = None
            for group in range(groups):
                term = lax.dot_general(
                    g_ref[half, group, row],
                    w_ref[group],
                    (((0,), (0,)), ((), ())),
                    preferred_element_type=jnp.float32,
                )
                total = term if total is None else total + term
            total = total.astype(jnp.bfloat16)
            first = lax.rem(lon[0] + half, 2) * (blocks // 2)
            for block in range(blocks):
                for k in range(basis):
                    mixed[
                        first + block // 2,
                        k * BLOCK : (k + 1) * BLOCK,
                        (block % 2) * LANES : (block % 2 + 1) * LANES,
                    ] = total[block * BLOCK : (block + 1) * BLOCK, k * LANES : (k + 1) * LANES]

        def multiply(pair, slot):
            piece[slot] = jnp.dot(t_ref[row], mixed[pair], preferred_element_type=jnp.float32)

        def put(pair, slot):
            for entry in range(entries):
                for side in range(2):
                    place = lax.rem(2 * pair + side + shift[row, entry], cycle_blocks)
                    acc[target[row, entry], place] += piece[
                        slot,
                        entry * BLOCK : (entry + 1) * BLOCK,
                        side * LANES : (side + 1) * LANES,
                    ]

        multiply(0, 0)

        @pl.loop(0, pairs // 2 - 1)
        def _(step):
            multiply(2 * step + 1, 1)
            put(2 * step, 0)
            multiply(2 * step + 2, 0)
            put(2 * step + 1, 1)

        multiply(pairs - 1, 1)
        put(pairs - 2, 0)
        put(pairs - 1, 1)

    steps = window // rows
    mid = steps // 2
    saves = []
    for step in sorted(range(steps), key=lambda at: -abs(at - mid)):
        far = step - (step > mid)
        for side in range(2):
            half = lax.rem(lon[0] + side, 2)
            for row in range(rows):
                block = acc[step * rows + row, pl.ds(half * blocks, blocks)]
                turned = block.reshape(width, LANES).T[:own_half]
                if step == mid:
                    near_ref[side, row] = turned
                else:
                    far_ref[far, side, row] = turned.astype(jnp.bfloat16)
            if step == mid:
                save = pltpu.make_async_copy(near_ref.at[side], near_hbm.at[side], store.at[step, side])
            else:
                save = pltpu.make_async_copy(
                    far_ref.at[far, side], far_hbm.at[far, side], store.at[step, side]
                )
            save.start()
            saves.append(save)
    for save in saves:
        save.wait()


def quadrature(own_half, target, shift, lon, g, w, t, window):
    lon_halves, groups, rows, channels, width = g.shape
    cycle_blocks = lon_halves * width // BLOCK
    depth = t.shape[2]
    vmem = pl.BlockSpec(memory_space=pltpu.VMEM)
    smem = pl.BlockSpec(memory_space=pltpu.SMEM)
    return pl.pallas_call(
        functools.partial(quadrature_kernel, own_half),
        out_shape=(
            jax.ShapeDtypeStruct(
                (window // rows - 1, 2, rows, own_half, width), jnp.bfloat16
            ),
            jax.ShapeDtypeStruct((2, rows, own_half, width), jnp.float32),
        ),
        in_specs=[smem, smem, smem, vmem, vmem, vmem],
        out_specs=(pl.BlockSpec(memory_space=pl.ANY), pl.BlockSpec(memory_space=pl.ANY)),
        scratch_shapes=[
            pltpu.VMEM((window // rows - 1, 2, rows, own_half, width), jnp.bfloat16),
            pltpu.VMEM((2, rows, own_half, width), jnp.float32),
            pltpu.VMEM((groups, channels, w.shape[0] * LANES), jnp.bfloat16),
            pltpu.VMEM((window + 1, cycle_blocks, BLOCK, LANES), jnp.float32),
            pltpu.VMEM((cycle_blocks // 2, depth, 2 * LANES), jnp.bfloat16),
            pltpu.VMEM((2, t.shape[1], 2 * LANES), jnp.float32),
            pltpu.SemaphoreType.DMA((window // rows, 2)),
        ],
        compiler_params=pltpu.CompilerParams(vmem_limit_bytes=36 * MIB),
        cost_estimate=pl.CostEstimate(
            flops=9 * 10**9, bytes_accessed=10 * 2**20, transcendentals=0
        ),
    )(target, shift, lon, g, w, t)


def filter_gradient(full_out, saved_basis):
    groups, rows, channels, width = full_out.shape
    basis = saved_basis.shape[0]
    lat_devices = lax.axis_size("lat")
    lon_devices = lax.axis_size("lon")
    own_rows = groups * channels // (lat_devices * lon_devices)
    if lat_devices > 8 or lon_devices != 2 or channels % (2 * own_rows):
        product = jnp.einsum(
            "crow,kirw->coki", full_out, saved_basis, preferred_element_type=jnp.float32
        )
        return lax.psum_scatter(
            product.reshape(groups * channels, basis, channels),
            ("lat", "lon"),
            scatter_dimension=0,
            tiled=True,
        )
    lat = lax.axis_index("lat")
    lon = lax.axis_index("lon")
    split = full_out.reshape(groups, rows, channels // (2 * own_rows), 2, own_rows, width)

    def half(which):
        product = jnp.einsum(
            "crlow,kirw->cloki",
            lax.dynamic_index_in_dim(split, which, 3, keepdims=False),
            saved_basis,
            preferred_element_type=jnp.float32,
        )
        return product.reshape(lat_devices, own_rows, basis, channels)

    received = lax.ppermute(half(1 - lon).astype(jnp.bfloat16), "lon", [(0, 1), (1, 0)])
    kept = half(lon)

    def both(step):
        at = lax.rem(lat + step, lat_devices)
        mine = lax.dynamic_index_in_dim(kept, at, 0, keepdims=False)
        return mine + lax.dynamic_index_in_dim(received, at, 0, keepdims=False)

    result = both(0)
    for step in range(1, lat_devices):
        result = result + lax.ppermute(
            both(step).astype(jnp.bfloat16),
            "lat",
            [(at, (at + step) % lat_devices) for at in range(lat_devices)],
        )
    return result


def body(grad_out, saved_basis, weight, quad_tiles, col_rows, col_shift, block_count):
    channels, rows, width = grad_out.shape
    entries = quad_tiles.shape[1]
    lat = lax.axis_index("lat")
    lon = lax.axis_index("lon")
    own_half = channels // 2
    window = (2 * HALO_DEV + 1) * rows

    whole_out, turned = gathered(grad_out.transpose(1, 0, 2), quad_tiles)
    grad_weight = filter_gradient(whole_out[0], saved_basis)
    live = jnp.arange(entries, dtype=jnp.int32)[None, :] < block_count[:, None]
    target = jnp.where(live, col_rows - (lat - HALO_DEV) * rows, window)
    far, near = quadrature(
        own_half, target, col_shift, lon[None].astype(jnp.int32), whole_out, weight.transpose(1, 0, 2), turned, window
    )

    grad_input = summed(far, near).transpose(1, 0, 2)
    return (grad_input, grad_weight)


def solution(mesh):
    in_specs = (
        P("ch", ("grp", "lat"), "lon"),
        P(None, "ch", ("grp", "lat"), "lon"),
        P(None, None, "ch"),
        P("lat", None, None, None, None),
        P("lat", None),
        P("lat", None),
        P("lat"),
    )
    out_specs = (P("ch", ("grp", "lat"), "lon"), P(("grp", "lat", "lon"), None, "ch"))
    return jax.shard_map(body, mesh=mesh, in_specs=in_specs, out_specs=out_specs, check_vma=False)
```
